512 devices in a mesh: dp: 32 (over z_lo, x), tensor: 16 (over z_hi, y, core).
Axes of the slice: x: 4, y: 4, z: 16 (z_hi: 2, z_lo: 8; z = z_hi * 8 + z_lo), core: 2. Of those that a mesh axis runs over, the one named last changes fastest.
Arguments:
- tokens: bfloat16 [8192, 3072], P('dp', 'tensor'), may hold values from -6 to 6
- tangent: bfloat16 [8192, 3072], P('dp', 'tensor'), may hold values from -6 to 6
- cotangent: bfloat16 [8192, 3072], P('dp', 'tensor'), may hold values from -6 to 6
- gates: float32 [8192], P('dp'), may hold values from 0.1 to 1
- slot_tokens: int32 [8192], P('dp'), may hold values from -1 to 255, as said below
- gate_weight: bfloat16 [3072, 8192], P('dp', 'tensor'), may hold values from -0.109375 to 0.109375
- up_weight: bfloat16 [3072, 8192], P('dp', 'tensor'), may hold values from -0.109375 to 0.109375
- down_weight: bfloat16 [8192, 3072], P('tensor', 'dp'), may hold values from -0.0625 to 0.0625
Outputs:
- hvp: bfloat16 [8192, 3072], P('dp', 'tensor')
The draws below stay inside these ranges and needn't reach their ends.
Inputs may be any that keep to these rules, and one draw needn't show every extreme that they name: `slot_tokens`: each group of 256 slots holds its live slots first, naming distinct tokens of that group in ascending order, and -1 in the rest; some group has all 256 slots live.
All inputs are finite; a program needn't handle non-finite values.
Results may differ from the reference program's by a relative error of at most 0.0049.
Values may be sent and summed in bfloat16 or wider, within the bound.
No kernel may reach another device: no remote copies, remote signals or barrier semaphores. Data moves between devices by JAX's collectives and lax.ppermute only.
A program may use at most 64 MiB of HBM per device.

```python
import jax
import jax.numpy as jnp
from jax import lax

D = 3072
FF = 8192
TOK_DEV = 256
ROWS = 256
TOKENS = 8192
N_DP = 32


def draw_slot_tokens(key, part):
    key = jax.random.fold_in(key, 11)
    keys = jax.random.split(key, N_DP + 2)
    counts = jax.random.randint(keys[0], (N_DP,), ROWS // 4, ROWS + 1)
    fullest = jax.random.randint(keys[1], (), 0, N_DP)
    counts = jnp.where(jnp.arange(N_DP) == fullest, ROWS, counts)

    def one_group(group_key, count):
        order = jax.random.permutation(group_key, TOK_DEV)
        chosen = jnp.zeros((TOK_DEV,), jnp.int32).at[order].set((jnp.arange(TOK_DEV) < count).astype(jnp.int32))
        ranked = jnp.argsort(1 - chosen, stable=True).astype(jnp.int32)
        return jnp.where(jnp.arange(ROWS) < count, ranked[:ROWS], -1)
    return jax.vmap(one_group)(keys[2:], counts).reshape(-1).astype(jnp.int32)


def block_levels(stream_key, extent, cuts, smallest, top_value):
    gain, own = 1.0, jax.random.fold_in(stream_key, 6)
    for dim, parts in cuts:
        draws = jnp.exp(jax.random.uniform(jax.random.fold_in(own, dim), (parts,), jnp.float32, smallest / len(cuts), top_value / len(cuts)))
        gain = gain * jnp.repeat(draws, extent[dim] // parts).reshape([-1 if axis == dim else 1 for axis in range(len(extent))])
    return gain


def centred(key, shape, spread, most, cuts=(), kind=jnp.bfloat16):
    values = spread * jax.random.normal(key, shape, jnp.float32)
    if cuts:
        values = values * block_levels(key, shape, cuts, -0.22, 0.18)
    return jnp.clip(values, -most, most).astype(kind)


def setup_inputs(seed: int = 0) -> dict:
    streams_of = jax.random.split(jax.random.key(seed), 9)
    tokens = centred(streams_of[0], (TOKENS, D), 1.0, 6.0, ((0, 32), (1, 16)))
    tangent = centred(streams_of[1], (TOKENS, D), 1.0, 6.0, ((0, 32), (1, 16)))
    cotangent = centred(streams_of[2], (TOKENS, D), 1.0, 6.0, ((0, 32), (1, 16)))
    gates = jnp.clip(0.1 + 0.9 * jax.random.uniform(streams_of[3], (TOKENS,), jnp.float32) ** block_levels(streams_of[3], (TOKENS,), ((0, 32),), -0.2, 0.2), 0.1, 1.0)
    slot_tokens = draw_slot_tokens(jax.random.fold_in(streams_of[8], 71), 0)
    gate_weight = centred(streams_of[5], (D, FF), D ** -0.5, 0.109375, ((0, 32), (1, 16)))
    up_weight = centred(streams_of[6], (D, FF), D ** -0.5, 0.109375, ((0, 32), (1, 16)))
    down_weight = centred(streams_of[7], (FF, D), FF ** -0.5, 0.0625, ((0, 16), (1, 32)))
    return dict(tokens=tokens, tangent=tangent, cotangent=cotangent, gates=gates, slot_tokens=slot_tokens, gate_weight=gate_weight, up_weight=up_weight, down_weight=down_weight)


def reference(tokens, tangent, cotangent, gates, slot_tokens, gate_weight, up_weight, down_weight):
    def one_group(items):
        inputs, tangents, cotangents, gate_row, slots = items
        live = slots >= 0
        index = jnp.maximum(slots, 0).astype(jnp.int32)
        zero_value = jnp.zeros((), inputs.dtype)
        picked_in = jnp.where(live[:, None], inputs[index], zero_value)
        picked_tan = jnp.where(live[:, None], tangents[index], zero_value)
        picked_cot = jnp.where(live[:, None], cotangents[index], zero_value)
        slot_gate = jnp.where(live, gate_row[index], jnp.zeros((), gate_row.dtype))
        gate_pre = jnp.dot(picked_in, gate_weight, preferred_element_type=jnp.float32)
        up_pre = jnp.dot(picked_in, up_weight, preferred_element_type=jnp.float32)
        gate_tan = jnp.dot(picked_tan, gate_weight, preferred_element_type=jnp.float32)
        up_tan = jnp.dot(picked_tan, up_weight, preferred_element_type=jnp.float32)
        back = slot_gate[:, None] * jnp.dot(picked_cot, down_weight.T, preferred_element_type=jnp.float32)
        squash = jax.nn.sigmoid(gate_pre)
        first = squash * (1.0 + gate_pre * (1.0 - squash))
        second = squash * (1.0 - squash) * (2.0 + gate_pre * (1.0 - 2.0 * squash))
        gate_dir = (back * (up_tan * first + up_pre * second * gate_tan)).astype(jnp.bfloat16)
        up_dir = (back * first * gate_tan).astype(jnp.bfloat16)
        slot_rows = jnp.dot(gate_dir, gate_weight.T, preferred_element_type=jnp.float32) + jnp.dot(up_dir, up_weight.T, preferred_element_type=jnp.float32)
        slot_rows = jnp.where(live[:, None], slot_rows, jnp.zeros((), slot_rows.dtype))
        result = jnp.zeros((TOK_DEV, D), slot_rows.dtype).at[index].add(slot_rows)
        return result.astype(jnp.bfloat16)

    result = lax.map(one_group, (tokens.reshape(N_DP, TOK_DEV, D), tangent.reshape(N_DP, TOK_DEV, D), cotangent.reshape(N_DP, TOK_DEV, D), gates.reshape(N_DP, TOK_DEV), slot_tokens.reshape(N_DP, ROWS)))
    return result.reshape(TOKENS, D)
```

```python
import jax
import jax.numpy as jnp
import numpy as np
from jax import lax
from jax.sharding import Mesh
from jax.sharding import PartitionSpec as P

BF = jnp.bfloat16
F32 = jnp.float32
NZ, NX, NH, NY, NC = 8, 4, 2, 4, 2
RING = (0, 2, 4, 6, 7, 5, 3, 1)


def shift(axis, order, step):
    n = len(order)
    pairs = [(order[i], order[(i + step) % n]) for i in range(n)]
    return lambda v: lax.ppermute(v, axis, pairs)


ring_up, ring_down = shift("zl", RING, 1), shift("zl", RING, -1)
x_up, x_down, x_far = (shift("x", range(NX), s) for s in (1, -1, 2))
y_up, y_down, y_far = (shift("y", range(NY), s) for s in (1, -1, 2))
other_half = shift("zh", range(NH), 1)
other_core = shift("c", range(NC), 1)


def take(v, i, axis=0):
    return lax.dynamic_index_in_dim(v, i, axis, keepdims=False)


def body(tokens, tangent, cotangent, gates, slot_tokens, gate_weight, up_weight, down_weight):
    zl, x, zh, y, c = (lax.axis_index(a) for a in ("zl", "x", "zh", "y", "c"))
    place = take(jnp.asarray(np.argsort(RING), jnp.int32), zl)
    ring = jnp.asarray(RING, jnp.int32)

    own = jnp.concatenate([gate_weight, up_weight, down_weight.T], axis=1)
    rows, width = own.shape
    half = rows // 2
    blocks = [(own[None], 0)]
    ups, downs = own, own
    rounds = [[(own, zl)]]
    for k in (1, 2, 3):
        ups, downs = ring_up(ups), ring_down(downs)
        rounds.append([(ups, take(ring, (place - k) % NZ)), (downs, take(ring, (place + k) % NZ))])
    last = jnp.concatenate([ring_up(ups[:half]), ring_down(downs[half:])], axis=0)
    rounds.append([(last, take(ring, (place + 4) % NZ))])

    fields = jnp.concatenate([tokens.T, tangent.T, cotangent.T], axis=1)
    feat, cols = fields.shape
    pair = jnp.stack([fields, other_half(fields)])
    pair = jnp.stack([take(pair, zh), take(pair, 1 - zh)])
    quad = jnp.zeros((NH, NY, feat, cols), BF)
    for part, src in ((pair, y), (y_up(pair), y - 1), (y_down(pair), y + 1), (y_far(pair), y + 2)):
        quad = lax.dynamic_update_slice(quad, part[:, None], (0, src % NY, 0, 0))
    across = other_core(quad)
    fields = jnp.zeros((NH, NY, NC, feat, cols), BF)
    fields = lax.dynamic_update_slice(fields, quad[:, :, None], (0, 0, c, 0, 0))
    fields = lax.dynamic_update_slice(fields, across[:, :, None], (0, 0, 1 - c, 0, 0))
    fields = fields.reshape(NH * NY * NC * feat, cols)

    full = jnp.zeros((NZ, NX, rows, width), BF)
    for group in rounds:
        for block, src in group:
            for part, at in ((block, x), (x_up(block), x - 1), (x_down(block), x + 1), (x_far(block), x + 2)):
                full = lax.dynamic_update_slice(full, part[None, None], (src, at % NX, 0, 0))
    full = full.reshape(NZ * NX * rows, width)

    n_tok = tokens.shape[0]
    ff = gate_weight.shape[1]
    both = full[:, : 2 * ff]
    pre = lax.dot_general(
        fields[:, : 2 * n_tok], both, (((0,), (0,)), ((), ())), preferred_element_type=F32
    )
    back = lax.dot_general(
        fields[:, 2 * n_tok :], full[:, 2 * ff :], (((0,), (0,)), ((), ())), preferred_element_type=F32
    )
    gate_pre, up_pre = pre[:n_tok, :ff], pre[:n_tok, ff:]
    gate_tan, up_tan = pre[n_tok:, :ff], pre[n_tok:, ff:]
    held = slot_tokens[:, None] == lax.broadcasted_iota(jnp.int32, (slot_tokens.shape[0], n_tok), 1)
    gate = jnp.where(jnp.any(held, axis=0), gates, 0.0)
    back = gate[:, None] * back
    squash = jax.nn.sigmoid(gate_pre)
    first = squash * (1.0 + gate_pre * (1.0 - squash))
    second = squash * (1.0 - squash) * (2.0 + gate_pre * (1.0 - 2.0 * squash))
    gate_dir = (back * (up_tan * first + up_pre * second * gate_tan)).astype(BF)
    up_dir = (back * first * gate_tan).astype(BF)
    dirs = jnp.concatenate([gate_dir, up_dir], axis=1)
    sums = lax.dot_general(both, dirs, (((1,), (1,)), ((), ())), preferred_element_type=F32)

    sums = sums.reshape(NH, NY, NC, feat, n_tok)
    sums = take(sums, c, 2) + other_core(take(sums, 1 - c, 2))

    def to(step):
        return take(sums, (y + step) % NY, 1)

    kept = to(0) + y_up(to(1).astype(BF)).astype(F32) + y_down(to(-1).astype(BF)).astype(F32)
    kept = kept + y_far(to(2).astype(BF)).astype(F32)
    out = take(kept, zh) + other_half(take(kept, 1 - zh).astype(BF)).astype(F32)
    return out.T.astype(BF)


def solution(mesh):
    fine = Mesh(mesh.devices.reshape(NZ, NX, NH, NY, NC), ("zl", "x", "zh", "y", "c"))
    dp, tensor = ("zl", "x"), ("zh", "y", "c")
    tok = P(dp, tensor)
    in_specs = (tok, tok, tok, P(dp), P(dp), tok, tok, P(tensor, dp))
    return jax.shard_map(body, mesh=fine, in_specs=in_specs, out_specs=tok, check_vma=False)
```

```python
import jax
import jax.numpy as jnp
import numpy as np
from jax import lax
from jax.sharding import Mesh
from jax.sharding import PartitionSpec as P

BF = jnp.bfloat16
F32 = jnp.float32
NZ, NX, NH, NY, NC = 8, 4, 2, 4, 2
RING = (0, 2, 4, 6, 7, 5, 3, 1)


def shift(axis, order, step):
    n = len(order)
    pairs = [(order[i], order[(i + step) % n]) for i in range(n)]
    return lambda v: lax.ppermute(v, axis, pairs)


ring_up, ring_down = shift("zl", RING, 1), shift("zl", RING, -1)
x_up, x_down, x_far = (shift("x", range(NX), s) for s in (1, -1, 2))
y_up, y_down, y_far = (shift("y", range(NY), s) for s in (1, -1, 2))
other_half = shift("zh", range(NH), 1)
other_core = shift("c", range(NC), 1)


def take(v, i, axis=0):
    return lax.dynamic_index_in_dim(v, i, axis, keepdims=False)


def body(tokens, tangent, cotangent, gates, slot_tokens, gate_weight, up_weight, down_weight):
    zl, x, zh, y, c = (lax.axis_index(a) for a in ("zl", "x", "zh", "y", "c"))
    place = take(jnp.asarray(np.argsort(RING), jnp.int32), zl)
    ring = jnp.asarray(RING, jnp.int32)

    fields = jnp.concatenate([tokens.T, tangent.T, cotangent.T], axis=1)
    feat = fields.shape[0]
    for axis in ("zh", "y", "c"):
        fields = lax.all_gather(fields, axis, axis=0, tiled=True)

    own = jnp.concatenate([gate_weight, up_weight, down_weight.T], axis=1)
    rows, width = own.shape
    ups, downs = own, own
    groups = [([own], [zl])]
    for k in (1, 2, 3):
        ups, downs = ring_up(ups), ring_down(downs)
        groups.append(([ups, downs], [take(ring, (place - k) % NZ), take(ring, (place + k) % NZ)]))
    groups.append(([ring_up(ups)], [take(ring, (place + 4) % NZ)]))

    full = jnp.zeros((NZ * NX * rows, width), BF)
    for blocks, sources in groups:
        sent = jnp.stack(blocks)
        for part, at in ((sent, x), (x_up(sent), x - 1), (x_down(sent), x + 1), (x_far(sent), x + 2)):
            at = at % NX
            for j, src in enumerate(sources):
                first_row = ((((at // 2) * NY + src % NY) * NH + src // NY) * 2 + at % 2) * rows
                full = lax.dynamic_update_slice(full, part[j], (first_row, 0))

    n_tok = tokens.shape[0]
    ff = gate_weight.shape[1]
    both = full[:, : 2 * ff]
    pre = lax.dot_general(
        fields[:, : 2 * n_tok], both, (((0,), (0,)), ((), ())), preferred_element_type=F32
    )
    back = lax.dot_general(
        fields[:, 2 * n_tok :], full[:, 2 * ff :], (((0,), (0,)), ((), ())), preferred_element_type=F32
    )
    gate_pre, up_pre = pre[:n_tok, :ff], pre[:n_tok, ff:]
    gate_tan, up_tan = pre[n_tok:, :ff], pre[n_tok:, ff:]
    held = slot_tokens[:, None] == lax.broadcasted_iota(jnp.int32, (slot_tokens.shape[0], n_tok), 1)
    gate = jnp.where(jnp.any(held, axis=0), gates, 0.0)
    back = gate[:, None] * back
    squash = jax.nn.sigmoid(gate_pre)
    first = squash * (1.0 + gate_pre * (1.0 - squash))
    second = squash * (1.0 - squash) * (2.0 + gate_pre * (1.0 - 2.0 * squash))
    gate_dir = (back * (up_tan * first + up_pre * second * gate_tan)).astype(BF)
    up_dir = (back * first * gate_tan).astype(BF)
    dirs = jnp.concatenate([gate_dir, up_dir], axis=1)
    sums = lax.dot_general(both, dirs, (((1,), (1,)), ((), ())), preferred_element_type=F32)

    sums = sums.reshape(NC, NY, NH, feat, n_tok)
    sums = take(sums, c) + other_core(take(sums, 1 - c))

    def to(step):
        return take(sums, (y + step) % NY)

    kept = to(0) + y_up(to(1).astype(BF)).astype(F32) + y_down(to(-1).astype(BF)).astype(F32)
    kept = kept + y_far(to(2).astype(BF)).astype(F32)
    out = take(kept, zh) + other_half(take(kept, 1 - zh).astype(BF)).astype(F32)
    return out.T.astype(BF)


def solution(mesh):
    fine = Mesh(mesh.devices.reshape(NZ, NX, NH, NY, NC), ("zl", "x", "zh", "y", "c"))
    dp, tensor = ("zl", "x"), ("zh", "y", "c")
    tok = P(dp, tensor)
    in_specs = (tok, tok, tok, P(dp), P(dp), tok, tok, P(tensor, dp))
    return jax.shard_map(body, mesh=fine, in_specs=in_specs, out_specs=tok, check_vma=False)
```

```python
import jax
import jax.numpy as jnp
import numpy as np
from jax import lax
from jax.sharding import Mesh
from jax.sharding import PartitionSpec as P

BF = jnp.bfloat16
F32 = jnp.float32
NZ, NX, NH, NY, NC = 8, 4, 2, 4, 2
RING = (0, 2, 4, 6, 7, 5, 3, 1)


def shift(axis, order, step):
    n = len(order)
    pairs = [(order[i], order[(i + step) % n]) for i in range(n)]
    return lambda v: lax.ppermute(v, axis, pairs)


ring_up, ring_down = shift("zl", RING, 1), shift("zl", RING, -1)
x_up, x_down, x_far = (shift("x", range(NX), s) for s in (1, -1, 2))


def flip(axis, n, bit):
    return lambda v: lax.ppermute(v, axis, [(i, i ^ bit) for i in range(n)])


y_near, y_far = flip("y", NY, 1), flip("y", NY, 2)
other_half = shift("zh", range(NH), 1)
other_core = shift("c", range(NC), 1)


def take(v, i, axis=0):
    return lax.dynamic_index_in_dim(v, i, axis, keepdims=False)


def body(tokens, tangent, cotangent, gates, slot_tokens, gate_weight, up_weight, down_weight):
    zl, x, zh, y, c = (lax.axis_index(a) for a in ("zl", "x", "zh", "y", "c"))
    place = take(jnp.asarray(np.argsort(RING), jnp.int32), zl)
    ring = jnp.asarray(RING, jnp.int32)

    own = jnp.concatenate([gate_weight, up_weight, down_weight.T], axis=1)
    rows, width = own.shape
    ups, downs = own, own
    groups = [([own], [zl])]
    for k in (1, 2, 3):
        ups, downs = ring_up(ups), ring_down(downs)
        groups.append(([ups, downs], [take(ring, (place - k) % NZ), take(ring, (place + k) % NZ)]))
    groups.append(([ring_up(ups)], [take(ring, (place + 4) % NZ)]))

    fields = jnp.concatenate([tokens.T, tangent.T, cotangent.T], axis=1)
    feat = fields.shape[0]

    def join(v, send, bit):
        got = send(v)
        return jnp.concatenate([jnp.where(bit == 0, v, got), jnp.where(bit == 0, got, v)])

    fields = join(fields, other_half, zh)
    fields = join(fields, y_near, y % 2)
    fields = join(fields, y_far, y // 2)
    fields = join(fields, other_core, c)

    full = jnp.zeros((NZ * NX * rows, width), BF)
    for blocks, sources in groups:
        sent = jnp.stack(blocks)
        late = sent
        if blocks[0] is own:
            late, _ = lax.optimization_barrier((sent, groups[1][0]))
        for part, at in ((sent, x), (x_up(sent), x - 1), (x_down(sent), x + 1), (x_far(late), x + 2)):
            at = at % NX
            for j, src in enumerate(sources):
                first_row = ((((at // 2) * NY + src % NY) * NH + src // NY) * 2 + at % 2) * rows
                full = lax.dynamic_update_slice(full, part[j], (first_row, 0))

    n_tok = tokens.shape[0]
    ff = gate_weight.shape[1]
    both = full[:, : 2 * ff]
    pre = lax.dot_general(
        fields[:, : 2 * n_tok], both, (((0,), (0,)), ((), ())), preferred_element_type=F32
    )
    back = lax.dot_general(
        fields[:, 2 * n_tok :], full[:, 2 * ff :], (((0,), (0,)), ((), ())), preferred_element_type=F32
    )
    gate_pre, up_pre = pre[:n_tok, :ff], pre[:n_tok, ff:]
    gate_tan, up_tan = pre[n_tok:, :ff], pre[n_tok:, ff:]
    held = slot_tokens[:, None] == lax.broadcasted_iota(jnp.int32, (slot_tokens.shape[0], n_tok), 1)
    gate = jnp.where(jnp.any(held, axis=0), gates, 0.0)
    back = gate[:, None] * back
    squash = jax.nn.sigmoid(gate_pre)
    first = squash * (1.0 + gate_pre * (1.0 - squash))
    second = squash * (1.0 - squash) * (2.0 + gate_pre * (1.0 - 2.0 * squash))
    gate_dir = (back * (up_tan * first + up_pre * second * gate_tan)).astype(BF)
    up_dir = (back * first * gate_tan).astype(BF)
    dirs = jnp.concatenate([gate_dir, up_dir], axis=1)
    sums = lax.dot_general(both, dirs, (((1,), (1,)), ((), ())), preferred_element_type=F32)

    sums = sums.reshape(NC, NY, NH, feat, n_tok)
    sums = take(sums, c) + other_core(take(sums, 1 - c))

    shares = lax.all_to_all(sums.astype(BF), "y", 0, 0, tiled=True).astype(F32)
    kept = jnp.sum(shares, axis=0)
    out = take(kept, zh) + other_half(take(kept, 1 - zh).astype(BF)).astype(F32)
    return out.T.astype(BF)


def solution(mesh):
    fine = Mesh(mesh.devices.reshape(NZ, NX, NH, NY, NC), ("zl", "x", "zh", "y", "c"))
    dp, tensor = ("zl", "x"), ("zh", "y", "c")
    tok = P(dp, tensor)
    in_specs = (tok, tok, tok, P(dp), P(dp), tok, tok, P(tensor, dp))
    return jax.shard_map(body, mesh=fine, in_specs=in_specs, out_specs=tok, check_vma=False)
```

```python
import jax
import jax.numpy as jnp
import numpy as np
from jax import lax
from jax.sharding import Mesh
from jax.sharding import PartitionSpec as P

BF = jnp.bfloat16
F32 = jnp.float32
NZ, NX, NH, NY, NC = 8, 4, 2, 4, 2
RING = (0, 2, 4, 6, 7, 5, 3, 1)
STEPS = (0, -1, 1, -2, 2, -3, 3, -4)
SOURCES = np.array(
    [sum(RING[(RING.index(z) + s) % NZ] << 3 * j for j, s in enumerate(STEPS)) for z in range(NZ)], np.uint32
)


def shift(axis, order, step):
    n = len(order)
    pairs = [(order[i], order[(i + step) % n]) for i in range(n)]
    return lambda v: lax.ppermute(v, axis, pairs)


ring_up, ring_down = shift("zl", RING, 1), shift("zl", RING, -1)
x_up, x_down, x_far = (shift("x", range(NX), s) for s in (1, -1, 2))


def flip(axis, n, bit):
    return lambda v: lax.ppermute(v, axis, [(i, i ^ bit) for i in range(n)])


y_near, y_far = flip("y", NY, 1), flip("y", NY, 2)
other_half = shift("zh", range(NH), 1)
other_core = shift("c", range(NC), 1)


def take(v, i, axis=0):
    return lax.dynamic_index_in_dim(v, i, axis, keepdims=False)


def body(tokens, tangent, cotangent, gates, slot_tokens, gate_weight, up_weight, down_weight):
    zl, x, zh, y, c = (lax.axis_index(a).astype(jnp.uint32) for a in ("zl", "x", "zh", "y", "c"))
    packed = take(jnp.asarray(SOURCES), zl)

    own = jnp.concatenate([gate_weight, up_weight, down_weight.T], axis=1)
    rows, width = own.shape
    ups, downs = own, own
    groups = [[own]]
    for _ in range(3):
        ups, downs = ring_up(ups), ring_down(downs)
        groups.append([ups, downs])
    groups.append([ring_up(ups)])

    fields = jnp.concatenate([tokens.T, tangent.T, cotangent.T], axis=1)
    feat = fields.shape[0]

    def join(v, send, bit):
        got = send(v)
        return jnp.concatenate([jnp.where(bit == 0, v, got), jnp.where(bit == 0, got, v)])

    fields = join(fields, other_half, zh)
    fields = join(fields, y_near, y & 1)
    fields = join(fields, y_far, y >> 1)
    fields = join(fields, other_core, c)

    zero = groups[2][0][0, 0] * 0
    full = jnp.broadcast_to(zero, (NC, NY, NH, 2, rows, width))
    none = jnp.uint32(0)
    sources = iter((((packed >> 3 * j) & 3, (packed >> 3 * j + 2) & 1) for j in range(NZ)))
    for blocks in groups:
        sent = jnp.stack(blocks)
        late = sent
        if blocks[0] is own:
            late, _ = lax.optimization_barrier((sent, groups[1][0]))
        parts = (sent, x_down(sent), x_far(late), x_up(sent))
        at = [next(sources) for _ in blocks]
        for step, part in enumerate(parts):
            col = x + step
            for j, (row, far) in enumerate(at):
                where = ((col >> 1) & 1, row, far, col & 1, none, none)
                full = lax.dynamic_update_slice(full, part[j][None, None, None, None], where)
    full = full.reshape(NZ * NX * rows, width)

    n_tok = tokens.shape[0]
    ff = gate_weight.shape[1]
    both = full[:, : 2 * ff]
    pre = lax.dot_general(
        fields[:, : 2 * n_tok], both, (((0,), (0,)), ((), ())), preferred_element_type=F32
    )
    back = lax.dot_general(
        fields[:, 2 * n_tok :], full[:, 2 * ff :], (((0,), (0,)), ((), ())), preferred_element_type=F32
    )
    gate_pre, up_pre = pre[:n_tok, :ff], pre[:n_tok, ff:]
    gate_tan, up_tan = pre[n_tok:, :ff], pre[n_tok:, ff:]
    held = slot_tokens[:, None] == lax.broadcasted_iota(jnp.int32, (slot_tokens.shape[0], n_tok), 1)
    gate = jnp.where(jnp.any(held, axis=0), gates, 0.0)
    back = gate[:, None] * back
    squash = jax.nn.sigmoid(gate_pre)
    first = squash * (1.0 + gate_pre * (1.0 - squash))
    second = squash * (1.0 - squash) * (2.0 + gate_pre * (1.0 - 2.0 * squash))
    gate_dir = (back * (up_tan * first + up_pre * second * gate_tan)).astype(BF)
    up_dir = (back * first * gate_tan).astype(BF)
    dirs = jnp.concatenate([gate_dir, up_dir], axis=1)
    sums = lax.dot_general(both, dirs, (((1,), (1,)), ((), ())), preferred_element_type=F32)

    sums = sums.reshape(NC, NY, NH, feat, n_tok)
    sums = take(sums, c) + other_core(take(sums, 1 - c))

    shares = lax.all_to_all(sums.astype(BF), "y", 0, 0, tiled=True).astype(F32)
    kept = jnp.sum(shares, axis=0)
    out = take(kept, zh) + other_half(take(kept, 1 - zh).astype(BF)).astype(F32)
    return out.T.astype(BF)


def solution(mesh):
    fine = Mesh(mesh.devices.reshape(NZ, NX, NH, NY, NC), ("zl", "x", "zh", "y", "c"))
    dp, tensor = ("zl", "x"), ("zh", "y", "c")
    tok = P(dp, tensor)
    in_specs = (tok, tok, tok, P(dp), P(dp), tok, tok, P(tensor, dp))
    return jax.shard_map(body, mesh=fine, in_specs=in_specs, out_specs=tok, check_vma=False)
```

```python
import jax
import jax.numpy as jnp
import numpy as np
from jax import lax
from jax.sharding import Mesh
from jax.sharding import PartitionSpec as P

BF = jnp.bfloat16
F32 = jnp.float32
NZ, NX, NH, NY, NC = 8, 4, 2, 4, 2
RING = (0, 2, 4, 6, 7, 5, 3, 1)
STEPS = (0, -1, 1, -2, 2, -3, 3, -4)
SOURCES = np.array(
    [sum(RING[(RING.index(z) + s) % NZ] << 3 * j for j, s in enumerate(STEPS)) for z in range(NZ)], np.uint32
)


def shift(axis, order, step):
    n = len(order)
    pairs = [(order[i], order[(i + step) % n]) for i in range(n)]
    return lambda v: lax.ppermute(v, axis, pairs)


ring_up, ring_down = shift("zl", RING, 1), shift("zl", RING, -1)
x_up, x_down, x_far = (shift("x", range(NX), s) for s in (1, -1, 2))


def flip(axis, n, bit):
    return lambda v: lax.ppermute(v, axis, [(i, i ^ bit) for i in range(n)])


y_near, y_far = flip("y", NY, 1), flip("y", NY, 2)
other_half = shift("zh", range(NH), 1)
other_core = shift("c", range(NC), 1)


def take(v, i, axis=0):
    return lax.dynamic_index_in_dim(v, i, axis, keepdims=False)


def after(v, *done):
    return lax.optimization_barrier((v, *done))[0]


def body(tokens, tangent, cotangent, gates, slot_tokens, gate_weight, up_weight, down_weight):
    zl, x, zh, y, c = (lax.axis_index(a).astype(jnp.uint32) for a in ("zl", "x", "zh", "y", "c"))
    packed = take(jnp.asarray(SOURCES), zl)

    own = jnp.concatenate([gate_weight, up_weight, down_weight.T], axis=1)
    rows, width = own.shape
    fields = jnp.concatenate([tokens.T, tangent.T, cotangent.T], axis=1)
    feat = fields.shape[0]

    def join(v, send, bit, *done):
        got = after(send(v), *done)
        return jnp.concatenate([jnp.where(bit == 0, v, got), jnp.where(bit == 0, got, v)])

    g0 = own[None]
    a1, b1 = ring_up(own), ring_down(own)
    p0, m0 = x_up(g0), x_down(g0)
    a2, b2 = ring_up(a1), ring_down(b1)
    g1 = jnp.stack([a1, b1])
    p1, m1 = x_up(after(g1, p0)), x_down(after(g1, m0))
    a3, b3 = ring_up(a2), ring_down(b2)
    f1 = x_far(after(g1, p1))
    f0 = x_far(after(g0, m1))
    g2 = jnp.stack([a2, b2])
    p2 = x_up(after(g2, a3))
    m2 = x_down(after(g2, b3))
    f2 = x_far(after(g2, f0))
    fields = join(fields, other_half, zh, b3)
    fields = join(fields, y_near, y & 1, p2)
    a4 = ring_up(after(a3, f1))
    g3 = jnp.stack([a3, b3])
    p3 = x_up(after(g3, p2))
    m3 = x_down(after(g3, m2))
    f3 = x_far(after(g3, f2))
    fields = join(fields, y_far, y >> 1, p3)
    g4 = a4[None]
    p4 = x_up(g4)
    m4 = x_down(after(g4, p3))
    f4 = x_far(after(g4, m3))
    fields = join(fields, other_core, c)

    zero = a2[0, 0] * 0
    full = jnp.broadcast_to(zero, (NC, NY, NH, 2, rows, width))
    none = jnp.uint32(0)
    sources = iter((((packed >> 3 * j) & 3, (packed >> 3 * j + 2) & 1) for j in range(NZ)))
    groups = ((g0, m0, f0, p0), (g1, m1, f1, p1), (g2, m2, f2, p2), (g3, m3, f3, p3), (g4, m4, f4, p4))
    for parts in groups:
        at = [next(sources) for _ in parts[0]]
        for step, part in enumerate(parts):
            col = x + step
            for j, (row, far) in enumerate(at):
                where = ((col >> 1) & 1, row, far, col & 1, none, none)
                full = lax.dynamic_update_slice(full, part[j][None, None, None, None], where)
    full = full.reshape(NZ * NX * rows, width)

    n_tok = tokens.shape[0]
    ff = gate_weight.shape[1]
    both = full[:, : 2 * ff]
    pre = lax.dot_general(
        fields[:, : 2 * n_tok], both, (((0,), (0,)), ((), ())), preferred_element_type=F32
    )
    back = lax.dot_general(
        fields[:, 2 * n_tok :], full[:, 2 * ff :], (((0,), (0,)), ((), ())), preferred_element_type=F32
    )
    gate_pre, up_pre = pre[:n_tok, :ff], pre[:n_tok, ff:]
    gate_tan, up_tan = pre[n_tok:, :ff], pre[n_tok:, ff:]
    held = slot_tokens[:, None] == lax.broadcasted_iota(jnp.int32, (slot_tokens.shape[0], n_tok), 1)
    gate = jnp.where(jnp.any(held, axis=0), gates, 0.0)
    back = gate[:, None] * back
    squash = jax.nn.sigmoid(gate_pre)
    first = squash * (1.0 + gate_pre * (1.0 - squash))
    second = squash * (1.0 - squash) * (2.0 + gate_pre * (1.0 - 2.0 * squash))
    gate_dir = (back * (up_tan * first + up_pre * second * gate_tan)).astype(BF)
    up_dir = (back * first * gate_tan).astype(BF)
    dirs = jnp.concatenate([gate_dir, up_dir], axis=1)
    sums = lax.dot_general(both, dirs, (((1,), (1,)), ((), ())), preferred_element_type=F32)

    sums = sums.reshape(NC, NY, NH, feat, n_tok)
    sums = take(sums, c) + other_core(take(sums, 1 - c))

    shares = lax.all_to_all(sums.astype(BF), "y", 0, 0, tiled=True).astype(F32)
    kept = jnp.sum(shares, axis=0)
    out = take(kept, zh) + other_half(take(kept, 1 - zh).astype(BF)).astype(F32)
    return out.T.astype(BF)


def solution(mesh):
    fine = Mesh(mesh.devices.reshape(NZ, NX, NH, NY, NC), ("zl", "x", "zh", "y", "c"))
    dp, tensor = ("zl", "x"), ("zh", "y", "c")
    tok = P(dp, tensor)
    in_specs = (tok, tok, tok, P(dp), P(dp), tok, tok, P(tensor, dp))
    return jax.shard_map(body, mesh=fine, in_specs=in_specs, out_specs=tok, check_vma=False)
```

```python
import jax
import jax.numpy as jnp
import numpy as np
from jax import lax
from jax.sharding import Mesh
from jax.sharding import PartitionSpec as P

BF = jnp.bfloat16
F32 = jnp.float32
NZ, NX, NH, NY, NC = 8, 4, 2, 4, 2
RING = (0, 2, 4, 6, 7, 5, 3, 1)
STEPS = (0, -1, 1, -2, 2, -3, 3, -4)
SOURCES = np.array(
    [sum(RING[(RING.index(z) + s) % NZ] << 3 * j for j, s in enumerate(STEPS)) for z in range(NZ)], np.uint32
)


def shift(axis, order, step):
    n = len(order)
    pairs = [(order[i], order[(i + step) % n]) for i in range(n)]
    return lambda v: lax.ppermute(v, axis, pairs)


ring_up, ring_down = shift("zl", RING, 1), shift("zl", RING, -1)
x_up, x_down, x_far = (shift("x", range(NX), s) for s in (1, -1, 2))


def flip(axis, n, bit):
    return lambda v: lax.ppermute(v, axis, [(i, i ^ bit) for i in range(n)])


y_near, y_far = flip("y", NY, 1), flip("y", NY, 2)
other_half = shift("zh", range(NH), 1)
other_core = shift("c", range(NC), 1)


def take(v, i, axis=0):
    return lax.dynamic_index_in_dim(v, i, axis, keepdims=False)


def after(v, *done):
    return lax.optimization_barrier((v, *done))[0]


def body(tokens, tangent, cotangent, gates, slot_tokens, gate_weight, up_weight, down_weight):
    zl, x, zh, y, c = (lax.axis_index(a).astype(jnp.uint32) for a in ("zl", "x", "zh", "y", "c"))

    own = jnp.concatenate([gate_weight, up_weight, down_weight.T], axis=1)
    rows, width = own.shape
    fields = jnp.concatenate([tokens.T, tangent.T, cotangent.T], axis=1)
    feat = fields.shape[0]

    def join(v, send, bit, *done):
        got = after(send(v), *done)
        return jnp.concatenate([jnp.where(bit == 0, v, got), jnp.where(bit == 0, got, v)])

    g0 = own[None]
    a1, b1 = ring_up(own), ring_down(own)
    p0, m0 = x_up(g0), x_down(g0)
    a2, b2 = ring_up(a1), ring_down(b1)
    g1 = jnp.stack([a1, b1])
    p1, m1 = x_up(after(g1, p0)), x_down(after(g1, m0))
    a3, b3 = ring_up(a2), ring_down(b2)
    f1 = x_far(after(g1, p1))
    f0 = x_far(after(g0, m1))
    g2 = jnp.stack([a2, b2])
    p2 = x_up(after(g2, a3))
    m2 = x_down(after(g2, b3))
    f2 = x_far(after(g2, f0))
    fields = join(fields, other_half, zh, m1, p1)
    fields = join(fields, y_near, y & 1, b3)
    a4 = ring_up(after(a3, f1))
    g3 = jnp.stack([a3, b3])
    p3 = x_up(after(g3, p2))
    m3 = x_down(after(g3, m2))
    f3 = x_far(after(g3, f2))
    fields = join(fields, y_far, y >> 1, m2)
    g4 = a4[None]
    p4 = x_up(g4)
    m4 = x_down(after(g4, p3))
    f4 = x_far(after(g4, m3))
    fields = join(fields, other_core, c)

    zero = f0[0, 0, 0] * 0
    full = jnp.broadcast_to(zero, (NC, NY, NH, 2, rows, width))
    none = jnp.uint32(0)
    zl, x, _ = lax.optimization_barrier((zl, x, f0))
    packed = take(jnp.asarray(SOURCES), zl)
    sources = iter((((packed >> 3 * j) & 3, (packed >> 3 * j + 2) & 1) for j in range(NZ)))
    groups = ((g0, m0, f0, p0), (g1, m1, f1, p1), (g2, m2, f2, p2), (g3, m3, f3, p3), (g4, m4, f4, p4))
    for parts in groups:
        at = [next(sources) for _ in parts[0]]
        for step, part in enumerate(parts):
            col = x + step
            for j, (row, far) in enumerate(at):
                where = ((col >> 1) & 1, row, far, col & 1, none, none)
                full = lax.dynamic_update_slice(full, part[j][None, None, None, None], where)
    full = full.reshape(NZ * NX * rows, width)

    n_tok = tokens.shape[0]
    ff = gate_weight.shape[1]
    both = full[:, : 2 * ff]
    pre = lax.dot_general(
        fields[:, : 2 * n_tok], both, (((0,), (0,)), ((), ())), preferred_element_type=F32
    )
    back = lax.dot_general(
        fields[:, 2 * n_tok :], full[:, 2 * ff :], (((0,), (0,)), ((), ())), preferred_element_type=F32
    )
    gate_pre, up_pre = pre[:n_tok, :ff], pre[:n_tok, ff:]
    gate_tan, up_tan = pre[n_tok:, :ff], pre[n_tok:, ff:]
    held = slot_tokens[:, None] == lax.broadcasted_iota(jnp.int32, (slot_tokens.shape[0], n_tok), 1)
    gate = jnp.where(jnp.any(held, axis=0), gates, 0.0)
    back = gate[:, None] * back
    squash = jax.nn.sigmoid(gate_pre)
    first = squash * (1.0 + gate_pre * (1.0 - squash))
    second = squash * (1.0 - squash) * (2.0 + gate_pre * (1.0 - 2.0 * squash))
    gate_dir = (back * (up_tan * first + up_pre * second * gate_tan)).astype(BF)
    up_dir = (back * first * gate_tan).astype(BF)
    dirs = jnp.concatenate([gate_dir, up_dir], axis=1)
    sums = lax.dot_general(both, dirs, (((1,), (1,)), ((), ())), preferred_element_type=F32)

    sums = sums.reshape(NC, NY, NH, feat, n_tok)
    sums = take(sums, c) + other_core(take(sums, 1 - c))

    shares = lax.all_to_all(sums.astype(BF), "y", 0, 0, tiled=True).astype(F32)
    kept = jnp.sum(shares, axis=0)
    out = take(kept, zh) + other_half(take(kept, 1 - zh).astype(BF)).astype(F32)
    return out.T.astype(BF)


def solution(mesh):
    fine = Mesh(mesh.devices.reshape(NZ, NX, NH, NY, NC), ("zl", "x", "zh", "y", "c"))
    dp, tensor = ("zl", "x"), ("zh", "y", "c")
    tok = P(dp, tensor)
    in_specs = (tok, tok, tok, P(dp), P(dp), tok, tok, P(tensor, dp))
    return jax.shard_map(body, mesh=fine, in_specs=in_specs, out_specs=tok, check_vma=False)
```

```python
import jax
import jax.numpy as jnp
import numpy as np
from jax import lax
from jax.sharding import Mesh
from jax.sharding import PartitionSpec as P

BF = jnp.bfloat16
F32 = jnp.float32
NZ, NX, NH, NY, NC = 8, 4, 2, 4, 2
RING = (0, 2, 4, 6, 7, 5, 3, 1)
STEPS = (0, -1, 1, -2, 2, -3, 3, -4)
SOURCES = np.array(
    [sum(RING[(RING.index(z) + s) % NZ] << 3 * j for j, s in enumerate(STEPS)) for z in range(NZ)], np.uint32
)


def shift(axis, order, step):
    n = len(order)
    pairs = [(order[i], order[(i + step) % n]) for i in range(n)]
    return lambda v: lax.ppermute(v, axis, pairs)


ring_up, ring_down = shift("zl", RING, 1), shift("zl", RING, -1)
x_up, x_down, x_far = (shift("x", range(NX), s) for s in (1, -1, 2))


def flip(axis, n, bit):
    return lambda v: lax.ppermute(v, axis, [(i, i ^ bit) for i in range(n)])


y_near, y_far = flip("y", NY, 1), flip("y", NY, 2)
other_half = shift("zh", range(NH), 1)
other_core = shift("c", range(NC), 1)


def take(v, i, axis=0):
    return lax.dynamic_index_in_dim(v, i, axis, keepdims=False)


def after(v, *done):
    return lax.optimization_barrier((v, *done))[0]


def body(tokens, tangent, cotangent, gates, slot_tokens, gate_weight, up_weight, down_weight):
    zl, x, zh, y, c = (lax.axis_index(a).astype(jnp.uint32) for a in ("zl", "x", "zh", "y", "c"))

    own = jnp.concatenate([gate_weight, up_weight, down_weight.T], axis=1)
    rows, width = own.shape
    half = rows // 2
    fields = jnp.concatenate([tokens.T, tangent.T, cotangent.T], axis=1)
    feat = fields.shape[0]

    def join(v, send, bit, *done):
        got = after(send(v), *done)
        return jnp.concatenate([jnp.where(bit == 0, v, got), jnp.where(bit == 0, got, v)])

    def pile(*blocks):
        return jnp.concatenate(blocks, axis=0)

    a1, b1 = ring_up(own), ring_down(own)
    p0, m0 = x_up(own), x_down(own)
    a2, b2 = ring_up(a1), ring_down(b1)
    g1 = pile(a1, b1)
    p1, m1 = x_up(after(g1, p0)), x_down(after(g1, m0))
    a3, b3 = ring_up(a2), ring_down(b2)
    p2 = x_up(after(pile(a2, b2, p0[:half]), p1))
    m2 = x_down(after(pile(a2, b2, m0[half:]), m1))
    fields = join(fields, other_half, zh, b3)
    fields = join(fields, y_near, y & 1, m2)
    a4 = ring_up(a3)
    g3 = pile(a3, b3)
    p3 = x_up(after(pile(a3, b3, p1[:rows]), p2))
    m3 = x_down(after(pile(a3, b3, m1[rows:]), m2))
    f3 = x_far(after(g3, a4))
    fields = join(fields, y_far, y >> 1, p3)
    p4 = x_up(after(pile(a4, p2[:rows]), p3))
    m4 = x_down(after(pile(a4, m2[rows : 2 * rows]), m3))
    f4 = x_far(after(a4, m3))
    fields = join(fields, other_core, c)

    zero = p3[0, 0] * 0
    full = jnp.broadcast_to(zero, (NC, NY, NH, 2, rows, width))
    none = jnp.uint32(0)
    none_yet = zero.astype(jnp.uint32)
    zl, x = zl + none_yet, x + none_yet
    packed = take(jnp.asarray(SOURCES), zl)
    lines = [((packed >> 3 * j) & 3, (packed >> 3 * j + 2) & 1) for j in range(NZ)]
    cols = [(((x + s) >> 1) & 1, (x + s) & 1) for s in range(NX)]
    pieces = [(own, 0, 0, 0), (m0, 0, 1, 0), (p0, 0, 3, 0), (p2[2 * rows :], 0, 2, 0), (m2[2 * rows :], 0, 2, half)]
    for k, parts in ((1, (g1, m1, p1)), (3, (pile(a2, b2), m2, p2)), (5, (g3, m3, p3))):
        for part, step in zip(parts, (0, 1, 3)):
            pieces += [(part[:rows], k, step, 0), (part[rows : 2 * rows], k + 1, step, 0)]
    pieces += [(p3[2 * rows :], 1, 2, 0), (m3[2 * rows :], 2, 2, 0), (f3[:rows], 5, 2, 0), (f3[rows:], 6, 2, 0)]
    pieces += [(p4[rows:], 3, 2, 0), (m4[rows:], 4, 2, 0)]
    pieces += [(a4, 7, 0, 0), (m4[:rows], 7, 1, 0), (p4[:rows], 7, 3, 0), (f4, 7, 2, 0)]
    for part, j, step, first in pieces:
        where = (cols[step][0], *lines[j], cols[step][1], jnp.uint32(first), none)
        full = lax.dynamic_update_slice(full, part[None, None, None, None], where)
    full = full.reshape(NZ * NX * rows, width)

    n_tok = tokens.shape[0]
    ff = gate_weight.shape[1]
    both = full[:, : 2 * ff]
    pre = lax.dot_general(
        fields[:, : 2 * n_tok], both, (((0,), (0,)), ((), ())), preferred_element_type=F32
    )
    back = lax.dot_general(
        fields[:, 2 * n_tok :], full[:, 2 * ff :], (((0,), (0,)), ((), ())), preferred_element_type=F32
    )
    gate_pre, up_pre = pre[:n_tok, :ff], pre[:n_tok, ff:]
    gate_tan, up_tan = pre[n_tok:, :ff], pre[n_tok:, ff:]
    held = slot_tokens[:, None] == lax.broadcasted_iota(jnp.int32, (slot_tokens.shape[0], n_tok), 1)
    gate = jnp.where(jnp.any(held, axis=0), gates, 0.0)
    back = gate[:, None] * back
    squash = jax.nn.sigmoid(gate_pre)
    first = squash * (1.0 + gate_pre * (1.0 - squash))
    second = squash * (1.0 - squash) * (2.0 + gate_pre * (1.0 - 2.0 * squash))
    gate_dir = (back * (up_tan * first + up_pre * second * gate_tan)).astype(BF)
    up_dir = (back * first * gate_tan).astype(BF)
    dirs = jnp.concatenate([gate_dir, up_dir], axis=1)
    sums = lax.dot_general(both, dirs, (((1,), (1,)), ((), ())), preferred_element_type=F32)

    sums = sums.reshape(NC, NY, NH, feat, n_tok)
    sums = take(sums, c) + other_core(take(sums, 1 - c))

    shares = lax.all_to_all(sums.astype(BF), "y", 0, 0, tiled=True).astype(F32)
    kept = jnp.sum(shares, axis=0)
    out = take(kept, zh) + other_half(take(kept, 1 - zh).astype(BF)).astype(F32)
    return out.T.astype(BF)


def solution(mesh):
    fine = Mesh(mesh.devices.reshape(NZ, NX, NH, NY, NC), ("zl", "x", "zh", "y", "c"))
    dp, tensor = ("zl", "x"), ("zh", "y", "c")
    tok = P(dp, tensor)
    in_specs = (tok, tok, tok, P(dp), P(dp), tok, tok, P(tensor, dp))
    return jax.shard_map(body, mesh=fine, in_specs=in_specs, out_specs=tok, check_vma=False)
```

```python
import jax
import jax.numpy as jnp
import numpy as np
from jax import lax
from jax.sharding import Mesh
from jax.sharding import PartitionSpec as P

BF = jnp.bfloat16
F32 = jnp.float32
NZ, NX, NH, NY, NC = 8, 4, 2, 4, 2
RING = (0, 2, 4, 6, 7, 5, 3, 1)
STEPS = (0, -1, 1, -2, 2, -3, 3, -4)


def offset_table(rows):
    table = np.zeros((NZ, NX, NZ * NX), np.uint32)
    for zl, x, j, s in np.ndindex(NZ, NX, NZ, NX):
        z, col = RING[(RING.index(zl) + STEPS[j]) % NZ], (x + s) % NX
        table[zl, x, j * NX + s] = ((((col // 2) * NY + z % NY) * NH + z // NY) * 2 + col % 2) * rows
    return table


def shift(axis, order, step):
    n = len(order)
    pairs = [(order[i], order[(i + step) % n]) for i in range(n)]
    return lambda v: lax.ppermute(v, axis, pairs)


ring_up, ring_down = shift("zl", RING, 1), shift("zl", RING, -1)
x_up, x_down, x_far = (shift("x", range(NX), s) for s in (1, -1, 2))


def flip(axis, n, bit):
    return lambda v: lax.ppermute(v, axis, [(i, i ^ bit) for i in range(n)])


y_near, y_far = flip("y", NY, 1), flip("y", NY, 2)
other_half = shift("zh", range(NH), 1)
other_core = shift("c", range(NC), 1)


def take(v, i, axis=0):
    return lax.dynamic_index_in_dim(v, i, axis, keepdims=False)


def after(v, *done):
    return lax.optimization_barrier((v, *done))[0]


def body(tokens, tangent, cotangent, gates, slot_tokens, gate_weight, up_weight, down_weight):
    zl, x, zh, y, c = (lax.axis_index(a).astype(jnp.uint32) for a in ("zl", "x", "zh", "y", "c"))

    own = jnp.concatenate([gate_weight, up_weight, down_weight.T], axis=1)
    rows, width = own.shape
    fields = jnp.concatenate([tokens.T, tangent.T, cotangent.T], axis=1)
    feat = fields.shape[0]

    def join(v, send, bit, *done):
        got = after(send(v), *done)
        return jnp.concatenate([jnp.where(bit == 0, v, got), jnp.where(bit == 0, got, v)])

    def pile(*blocks):
        return jnp.concatenate(blocks, axis=0)

    a1, b1 = ring_up(own), ring_down(own)
    p0, m0 = x_up(own), x_down(own)
    a2, b2 = ring_up(after(a1, p0)), ring_down(after(b1, m0))
    g1 = pile(a1, b1)
    p1, m1 = x_up(after(g1, p0)), x_down(after(g1, m0))
    a3, b3 = ring_up(a2), ring_down(b2)
    f0 = x_far(after(own, m1))
    m2 = x_down(after(pile(a2, b2, m1[rows:]), p1))
    p2 = x_up(after(pile(a2, b2, p1[:rows]), a3))
    fields = join(fields, other_half, zh, b3)
    fields = join(fields, y_near, y & 1, m2)
    g3 = pile(a3, b3)
    m3 = x_down(after(g3, b3))
    p3 = x_up(after(g3, f0))
    a4 = ring_up(after(a3, m2))
    f3 = x_far(after(g3, p2))
    fields = join(fields, y_far, y >> 1, p3)
    m4 = x_down(pile(a4, m2[rows : 2 * rows]))
    p4 = x_up(after(pile(a4, p2[:rows]), m3))
    f4 = x_far(after(a4, p3))
    fields = join(fields, other_core, c)

    zl, x, _ = lax.optimization_barrier((zl, x, m2))
    offsets = lax.dynamic_slice(jnp.asarray(offset_table(rows)), (zl, x, jnp.uint32(0)), (1, 1, NZ * NX)).reshape(-1)
    full = jnp.broadcast_to(m2[0, 0] * 0, (NZ * NX * rows, width))
    pieces = [(own, 0, 0), (m0, 0, 1), (f0, 0, 2), (p0, 0, 3)]
    for k, parts in ((1, (g1, m1, p1)), (3, (pile(a2, b2), m2, p2)), (5, (g3, m3, p3))):
        for part, step in zip(parts, (0, 1, 3)):
            pieces += [(part[:rows], k, step), (part[rows : 2 * rows], k + 1, step)]
    pieces += [(p2[2 * rows :], 1, 2), (m2[2 * rows :], 2, 2), (f3[:rows], 5, 2), (f3[rows:], 6, 2)]
    pieces += [(p4[rows:], 3, 2), (m4[rows:], 4, 2)]
    pieces += [(a4, 7, 0), (m4[:rows], 7, 1), (p4[:rows], 7, 3), (f4, 7, 2)]
    for part, j, step in pieces:
        at = j * NX + step
        first = lax.squeeze(lax.slice(offsets, (at,), (at + 1,)), (0,))
        full = lax.dynamic_update_slice(full, part, (first, jnp.uint32(0)))

    n_tok = tokens.shape[0]
    ff = gate_weight.shape[1]
    both = full[:, : 2 * ff]
    pre = lax.dot_general(
        fields[:, : 2 * n_tok], both, (((0,), (0,)), ((), ())), preferred_element_type=F32
    )
    back = lax.dot_general(
        fields[:, 2 * n_tok :], full[:, 2 * ff :], (((0,), (0,)), ((), ())), preferred_element_type=F32
    )
    gate_pre, up_pre = pre[:n_tok, :ff], pre[:n_tok, ff:]
    gate_tan, up_tan = pre[n_tok:, :ff], pre[n_tok:, ff:]
    held = slot_tokens[:, None] == lax.broadcasted_iota(jnp.int32, (slot_tokens.shape[0], n_tok), 1)
    gate = jnp.where(jnp.any(held, axis=0), gates, 0.0)
    back = gate[:, None] * back
    squash = jax.nn.sigmoid(gate_pre)
    first = squash * (1.0 + gate_pre * (1.0 - squash))
    second = squash * (1.0 - squash) * (2.0 + gate_pre * (1.0 - 2.0 * squash))
    gate_dir = (back * (up_tan * first + up_pre * second * gate_tan)).astype(BF)
    up_dir = (back * first * gate_tan).astype(BF)
    dirs = jnp.concatenate([gate_dir, up_dir], axis=1)
    sums = lax.dot_general(both, dirs, (((1,), (1,)), ((), ())), preferred_element_type=F32)

    sums = sums.reshape(NC, NY, NH, feat, n_tok)
    sums = take(sums, c) + other_core(take(sums, 1 - c))

    shares = lax.all_to_all(sums.astype(BF), "y", 0, 0, tiled=True).astype(F32)
    kept = jnp.sum(shares, axis=0)
    out = take(kept, zh) + other_half(take(kept, 1 - zh).astype(BF)).astype(F32)
    return out.T.astype(BF)


def solution(mesh):
    fine = Mesh(mesh.devices.reshape(NZ, NX, NH, NY, NC), ("zl", "x", "zh", "y", "c"))
    dp, tensor = ("zl", "x"), ("zh", "y", "c")
    tok = P(dp, tensor)
    in_specs = (tok, tok, tok, P(dp), P(dp), tok, tok, P(tensor, dp))
    return jax.shard_map(body, mesh=fine, in_specs=in_specs, out_specs=tok, check_vma=False)
```

```python
import jax
import jax.numpy as jnp
import numpy as np
from jax import lax
from jax.sharding import Mesh
from jax.sharding import PartitionSpec as P

BF = jnp.bfloat16
F32 = jnp.float32
NZ, NX, NH, NY, NC = 8, 4, 2, 4, 2
RING = (0, 2, 4, 6, 7, 5, 3, 1)
STEPS = (0, -1, 1, -2, 2, -3, 3, -4)


def block_table():
    table = np.zeros((NZ, NX, NZ * NX), np.uint32)
    for zl, x, j, s in np.ndindex(NZ, NX, NZ, NX):
        z, col = RING[(RING.index(zl) + STEPS[j]) % NZ], (x + s) % NX
        table[zl, x, j * NX + s] = (((col // 2) * NY + z % NY) * NH + z // NY) * 2 + col % 2
    return table


def shift(axis, order, step):
    n = len(order)
    pairs = [(order[i], order[(i + step) % n]) for i in range(n)]
    return lambda v: lax.ppermute(v, axis, pairs)


ring_up, ring_down = shift("zl", RING, 1), shift("zl", RING, -1)
x_up, x_down, x_far = (shift("x", range(NX), s) for s in (1, -1, 2))


def flip(axis, n, bit):
    return lambda v: lax.ppermute(v, axis, [(i, i ^ bit) for i in range(n)])


y_near, y_far = flip("y", NY, 1), flip("y", NY, 2)
other_half = shift("zh", range(NH), 1)
other_core = shift("c", range(NC), 1)


def take(v, i, axis=0):
    return lax.dynamic_index_in_dim(v, i, axis, keepdims=False)


def after(v, *done):
    return lax.optimization_barrier((v, *done))[0]


def body(tokens, tangent, cotangent, gates, slot_tokens, gate_weight, up_weight, down_weight):
    zl, x, zh, y, c = (lax.axis_index(a).astype(jnp.uint32) for a in ("zl", "x", "zh", "y", "c"))

    own = jnp.concatenate([gate_weight, up_weight, down_weight.T], axis=1)
    rows, width = own.shape
    fields = jnp.concatenate([tokens.T, tangent.T, cotangent.T], axis=1)
    feat = fields.shape[0]

    def join(v, send, bit, *done):
        got = after(send(v), *done)
        return jnp.concatenate([jnp.where(bit == 0, v, got), jnp.where(bit == 0, got, v)])

    def pile(*blocks):
        return jnp.concatenate(blocks, axis=0)

    a1, b1 = ring_up(own), ring_down(own)
    p0, m0 = x_up(own), x_down(own)
    a2, b2 = ring_up(after(a1, p0)), ring_down(after(b1, m0))
    g1 = pile(a1, b1)
    p1, m1 = x_up(after(g1, p0)), x_down(after(g1, m0))
    a3, b3 = ring_up(a2), ring_down(b2)
    f0 = x_far(after(own, a3))
    m2 = x_down(pile(a2, b2, m1[rows:]))
    p2 = x_up(pile(a2, b2, p1[:rows]))
    fields = join(fields, other_half, zh, b3)
    fields = join(fields, y_near, y & 1, m2)
    g3 = pile(a3, b3)
    m3 = x_down(after(g3, m2))
    p3 = x_up(after(g3, p2))
    a4 = ring_up(a3)
    f3 = x_far(after(g3, f0))
    fields = join(fields, y_far, y >> 1, p3)
    m4 = x_down(pile(a4, m2[rows : 2 * rows]))
    p4 = x_up(after(pile(a4, p2[:rows]), m3))
    f4 = x_far(after(a4, p3))
    fields = join(fields, other_core, c)

    zl, x, _ = lax.optimization_barrier((zl, x, m2))
    offsets = lax.dynamic_slice(jnp.asarray(block_table()), (zl, x, jnp.uint32(0)), (1, 1, NZ * NX)).reshape(-1)
    full = jnp.broadcast_to(m2[0, 0] * 0, (NZ * NX, rows, width))
    pieces = [(own, 0, 0), (m0, 0, 1), (f0, 0, 2), (p0, 0, 3)]
    for k, parts in ((1, (g1, m1, p1)), (3, (pile(a2, b2), m2, p2)), (5, (g3, m3, p3))):
        for part, step in zip(parts, (0, 1, 3)):
            pieces += [(part[:rows], k, step), (part[rows : 2 * rows], k + 1, step)]
    pieces += [(p2[2 * rows :], 1, 2), (m2[2 * rows :], 2, 2), (f3[:rows], 5, 2), (f3[rows:], 6, 2)]
    pieces += [(p4[rows:], 3, 2), (m4[rows:], 4, 2)]
    pieces += [(a4, 7, 0), (m4[:rows], 7, 1), (p4[:rows], 7, 3), (f4, 7, 2)]
    none = jnp.uint32(0)
    for part, j, step in pieces:
        at = j * NX + step
        first = lax.squeeze(lax.slice(offsets, (at,), (at + 1,)), (0,))
        full = lax.dynamic_update_slice(full, part[None], (first, none, none))
    full = full.reshape(NZ * NX * rows, width)

    n_tok = tokens.shape[0]
    ff = gate_weight.shape[1]
    both = full[:, : 2 * ff]
    pre = lax.dot_general(
        fields[:, : 2 * n_tok], both, (((0,), (0,)), ((), ())), preferred_element_type=F32
    )
    back = lax.dot_general(
        fields[:, 2 * n_tok :], full[:, 2 * ff :], (((0,), (0,)), ((), ())), preferred_element_type=F32
    )
    gate_pre, up_pre = pre[:n_tok, :ff], pre[:n_tok, ff:]
    gate_tan, up_tan = pre[n_tok:, :ff], pre[n_tok:, ff:]
    held = slot_tokens[:, None] == lax.broadcasted_iota(jnp.int32, (slot_tokens.shape[0], n_tok), 1)
    gate = jnp.where(jnp.any(held, axis=0), gates, 0.0)
    back = gate[:, None] * back
    squash = jax.nn.sigmoid(gate_pre)
    first = squash * (1.0 + gate_pre * (1.0 - squash))
    second = squash * (1.0 - squash) * (2.0 + gate_pre * (1.0 - 2.0 * squash))
    gate_dir = (back * (up_tan * first + up_pre * second * gate_tan)).astype(BF)
    up_dir = (back * first * gate_tan).astype(BF)
    dirs = jnp.concatenate([gate_dir, up_dir], axis=1)
    sums = lax.dot_general(both, dirs, (((1,), (1,)), ((), ())), preferred_element_type=F32)

    sums = sums.reshape(NC, NY, NH, feat, n_tok)
    sums = take(sums, c) + other_core(take(sums, 1 - c))

    shares = lax.all_to_all(sums.astype(BF), "y", 0, 0, tiled=True).astype(F32)
    kept = jnp.sum(shares, axis=0)
    out = take(kept, zh) + other_half(take(kept, 1 - zh).astype(BF)).astype(F32)
    return out.T.astype(BF)


def solution(mesh):
    fine = Mesh(mesh.devices.reshape(NZ, NX, NH, NY, NC), ("zl", "x", "zh", "y", "c"))
    dp, tensor = ("zl", "x"), ("zh", "y", "c")
    tok = P(dp, tensor)
    in_specs = (tok, tok, tok, P(dp), P(dp), tok, tok, P(tensor, dp))
    return jax.shard_map(body, mesh=fine, in_specs=in_specs, out_specs=tok, check_vma=False)
```

```python
import jax
import jax.numpy as jnp
import numpy as np
from jax import lax
from jax.sharding import Mesh
from jax.sharding import PartitionSpec as P

BF = jnp.bfloat16
F32 = jnp.float32
NZ, NX, NH, NY, NC = 8, 4, 2, 4, 2
RING = (0, 2, 4, 6, 7, 5, 3, 1)
STEPS = (0, -1, 1, -2, 2, -3, 3, -4)


PLACES = np.zeros((NZ, NX, 2 * NZ + 2 * NX), np.uint32)
for zl_, x_ in np.ndindex(NZ, NX):
    rings = [RING[(RING.index(zl_) + step) % NZ] for step in STEPS]
    at = [v for z in rings for v in (z % NY, z // NY)]
    PLACES[zl_, x_] = at + [v for step in range(NX) for v in ((x_ + step) % NX // 2, (x_ + step) % 2)]


def shift(axis, order, step):
    n = len(order)
    pairs = [(order[i], order[(i + step) % n]) for i in range(n)]
    return lambda v: lax.ppermute(v, axis, pairs)


ring_up, ring_down = shift("zl", RING, 1), shift("zl", RING, -1)
x_up, x_down, x_far = (shift("x", range(NX), s) for s in (1, -1, 2))


def flip(axis, n, bit):
    return lambda v: lax.ppermute(v, axis, [(i, i ^ bit) for i in range(n)])


y_near, y_far = flip("y", NY, 1), flip("y", NY, 2)
other_half = shift("zh", range(NH), 1)
other_core = shift("c", range(NC), 1)


def take(v, i, axis=0):
    return lax.dynamic_index_in_dim(v, i, axis, keepdims=False)


def after(v, *done):
    return lax.optimization_barrier((v, *done))[0]


def body(tokens, tangent, cotangent, gates, slot_tokens, gate_weight, up_weight, down_weight):
    zl, x, zh, y, c = (lax.axis_index(a).astype(jnp.uint32) for a in ("zl", "x", "zh", "y", "c"))

    own = jnp.concatenate([gate_weight, up_weight, down_weight.T], axis=1)
    rows, width = own.shape
    fields = jnp.concatenate([tokens.T, tangent.T, cotangent.T], axis=1)
    feat = fields.shape[0]

    def join(v, send, bit, *done):
        got = after(send(v), *done)
        return jnp.concatenate([jnp.where(bit == 0, v, got), jnp.where(bit == 0, got, v)])

    a1, b1 = ring_up(own), ring_down(own)
    p0, m0 = x_up(own[None]), x_down(own[None])
    a2, b2 = ring_up(after(a1, p0)), ring_down(after(b1, m0))
    g1 = jnp.stack([a1, b1])
    p1, m1 = x_up(after(g1, p0)), x_down(after(g1, m0))
    a3, b3 = ring_up(a2), ring_down(b2)
    f0 = x_far(after(own[None], a3))
    m2 = x_down(jnp.stack([a2, b2, m1[1]]))
    p2 = x_up(jnp.stack([a2, b2, p1[0]]))
    fields = join(fields, other_half, zh, b3)
    fields = join(fields, y_near, y & 1, m2)
    g3 = jnp.stack([a3, b3])
    m3 = x_down(after(g3, m2))
    p3 = x_up(after(g3, p2))
    a4 = ring_up(a3)
    f3 = x_far(after(g3, f0))
    fields = join(fields, y_far, y >> 1, p3)
    m4 = x_down(jnp.stack([a4, m2[1]]))
    p4 = x_up(after(jnp.stack([a4, p2[0]]), m3))
    f4 = x_far(after(a4[None], p3))
    fields = join(fields, other_core, c)

    zl, x, _ = lax.optimization_barrier((zl, x, m2))
    places = lax.dynamic_slice(jnp.asarray(PLACES), (zl, x, jnp.uint32(0)), (1, 1, PLACES.shape[2])).reshape(-1)

    def place(i):
        return lax.squeeze(lax.slice(places, (i,), (i + 1,)), (0,))

    lines = [(place(2 * j), place(2 * j + 1)) for j in range(NZ)]
    cols = [(place(2 * NZ + 2 * step), place(2 * NZ + 2 * step + 1)) for step in range(NX)]
    none = jnp.uint32(0)
    full = jnp.broadcast_to(p3[0, 0, 0] * 0, (NC, NY, NH, 2, rows, width))
    pieces = [(own, 0, 0), (m0[0], 0, 1), (p0[0], 0, 3)]
    for k, parts in ((1, (g1, m1, p1)), (3, (jnp.stack([a2, b2]), m2, p2))):
        for part, step in zip(parts, (0, 1, 3)):
            pieces += [(part[0], k, step), (part[1], k + 1, step)]
    pieces += [(p2[2], 1, 2), (m2[2], 2, 2), (f0[0], 0, 2)]
    for part, step in ((g3, 0), (m3, 1), (p3, 3), (f3, 2)):
        pieces += [(part[0], 5, step), (part[1], 6, step)]
    pieces += [(p4[1], 3, 2), (m4[1], 4, 2)]
    pieces += [(a4, 7, 0), (m4[0], 7, 1), (p4[0], 7, 3), (f4[0], 7, 2)]
    for part, j, step in pieces:
        where = (cols[step][0], *lines[j], cols[step][1], none, none)
        full = lax.dynamic_update_slice(full, part[None, None, None, None], where)
    full = full.reshape(NZ * NX * rows, width)

    n_tok = tokens.shape[0]
    ff = gate_weight.shape[1]
    both = full[:, : 2 * ff]
    pre = lax.dot_general(
        fields[:, : 2 * n_tok], both, (((0,), (0,)), ((), ())), preferred_element_type=F32
    )
    back = lax.dot_general(
        fields[:, 2 * n_tok :], full[:, 2 * ff :], (((0,), (0,)), ((), ())), preferred_element_type=F32
    )
    gate_pre, up_pre = pre[:n_tok, :ff], pre[:n_tok, ff:]
    gate_tan, up_tan = pre[n_tok:, :ff], pre[n_tok:, ff:]
    held = slot_tokens[:, None] == lax.broadcasted_iota(jnp.int32, (slot_tokens.shape[0], n_tok), 1)
    gate = jnp.where(jnp.any(held, axis=0), gates, 0.0)
    back = gate[:, None] * back
    squash = jax.nn.sigmoid(gate_pre)
    first = squash * (1.0 + gate_pre * (1.0 - squash))
    second = squash * (1.0 - squash) * (2.0 + gate_pre * (1.0 - 2.0 * squash))
    gate_dir = (back * (up_tan * first + up_pre * second * gate_tan)).astype(BF)
    up_dir = (back * first * gate_tan).astype(BF)
    dirs = jnp.concatenate([gate_dir, up_dir], axis=1)
    sums = lax.dot_general(both, dirs, (((1,), (1,)), ((), ())), preferred_element_type=F32)

    sums = sums.reshape(NC, NY, NH, feat, n_tok)
    sums = take(sums, c) + other_core(take(sums, 1 - c))

    shares = lax.all_to_all(sums.astype(BF), "y", 0, 0, tiled=True).astype(F32)
    kept = jnp.sum(shares, axis=0)
    out = take(kept, zh) + other_half(take(kept, 1 - zh).astype(BF)).astype(F32)
    return out.T.astype(BF)


def solution(mesh):
    fine = Mesh(mesh.devices.reshape(NZ, NX, NH, NY, NC), ("zl", "x", "zh", "y", "c"))
    dp, tensor = ("zl", "x"), ("zh", "y", "c")
    tok = P(dp, tensor)
    in_specs = (tok, tok, tok, P(dp), P(dp), tok, tok, P(tensor, dp))
    return jax.shard_map(body, mesh=fine, in_specs=in_specs, out_specs=tok, check_vma=False)
```

```python
import jax
import jax.numpy as jnp
import numpy as np
from jax import lax
from jax.sharding import Mesh
from jax.sharding import PartitionSpec as P

BF = jnp.bfloat16
F32 = jnp.float32
NZ, NX, NH, NY, NC = 8, 4, 2, 4, 2
RING = (0, 2, 4, 6, 7, 5, 3, 1)
STEPS = (0, -1, 1, -2, 2, -3, 3, -4)
PLACES = np.array(
    [
        [
            [v for s in STEPS for z in [RING[(RING.index(zl) + s) % NZ]] for v in (z % NY, z // NY)]
            + [v for s in range(NX) for v in ((x + s) % NX // 2, (x + s) % 2)]
            for x in range(NX)
        ]
        for zl in range(NZ)
    ],
    np.uint32,
)


def shift(axis, order, step):
    n = len(order)
    pairs = [(order[i], order[(i + step) % n]) for i in range(n)]
    return lambda v: lax.ppermute(v, axis, pairs)


ring_up, ring_down = shift("zl", RING, 1), shift("zl", RING, -1)
x_up, x_down, x_far = (shift("x", range(NX), s) for s in (1, -1, 2))


def flip(axis, n, bit):
    return lambda v: lax.ppermute(v, axis, [(i, i ^ bit) for i in range(n)])


y_near, y_far = flip("y", NY, 1), flip("y", NY, 2)
other_half = shift("zh", range(NH), 1)
other_core = shift("c", range(NC), 1)


def take(v, i, axis=0):
    return lax.dynamic_index_in_dim(v, i, axis, keepdims=False)


def after(v, *done):
    return lax.optimization_barrier((v, *done))[0]


def body(tokens, tangent, cotangent, gates, slot_tokens, gate_weight, up_weight, down_weight):
    zl, x, zh, y, c = (lax.axis_index(a).astype(jnp.uint32) for a in ("zl", "x", "zh", "y", "c"))
    places = lax.dynamic_slice(jnp.asarray(PLACES), (zl, x, jnp.uint32(0)), (1, 1, PLACES.shape[2])).reshape(-1)

    def place(i):
        return lax.squeeze(lax.slice(places, (i,), (i + 1,)), (0,))


    own = jnp.concatenate([gate_weight, up_weight, down_weight.T], axis=1)
    rows, width = own.shape
    fields = jnp.concatenate([tokens.T, tangent.T, cotangent.T], axis=1)
    feat = fields.shape[0]

    def join(v, send, bit, *done):
        got = after(send(v), *done)
        return jnp.concatenate([jnp.where(bit == 0, v, got), jnp.where(bit == 0, got, v)])

    g0 = own[None]
    a1, b1 = ring_up(own), ring_down(own)
    p0, m0 = x_up(g0), x_down(g0)
    a2, b2 = ring_up(a1), ring_down(b1)
    g1 = jnp.stack([a1, b1])
    p1, m1 = x_up(after(g1, p0)), x_down(after(g1, m0))
    a3, b3 = ring_up(a2), ring_down(b2)
    f1 = x_far(after(g1, p1))
    f0 = x_far(after(g0, m1))
    g2 = jnp.stack([a2, b2])
    p2 = x_up(after(g2, a3))
    m2 = x_down(after(g2, b3))
    f2 = x_far(after(g2, f0))
    fields = join(fields, other_half, zh, b3)
    fields = join(fields, y_near, y & 1, p2)
    a4 = ring_up(after(a3, f1))
    g3 = jnp.stack([a3, b3])
    p3 = x_up(after(g3, p2))
    m3 = x_down(after(g3, m2))
    f3 = x_far(after(g3, f2))
    fields = join(fields, y_far, y >> 1, p3)
    g4 = a4[None]
    p4 = x_up(g4)
    m4 = x_down(after(g4, p3))
    f4 = x_far(after(g4, m3))
    fields = join(fields, other_core, c)

    zero = a2[0, 0] * 0
    full = jnp.broadcast_to(zero, (NC, NY, NH, 2, rows, width))
    none = jnp.uint32(0)
    sources = iter([(place(2 * j), place(2 * j + 1)) for j in range(NZ)])
    cols = [(place(2 * NZ + 2 * s), place(2 * NZ + 2 * s + 1)) for s in range(NX)]
    groups = ((g0, m0, f0, p0), (g1, m1, f1, p1), (g2, m2, f2, p2), (g3, m3, f3, p3), (g4, m4, f4, p4))
    for parts in groups:
        at = [next(sources) for _ in parts[0]]
        for step, part in enumerate(parts):
            for j, (row, far) in enumerate(at):
                where = (cols[step][0], row, far, cols[step][1], none, none)
                full = lax.dynamic_update_slice(full, part[j][None, None, None, None], where)
    full = full.reshape(NZ * NX * rows, width)

    n_tok = tokens.shape[0]
    ff = gate_weight.shape[1]
    both = full[:, : 2 * ff]
    pre = lax.dot_general(
        fields[:, : 2 * n_tok], both, (((0,), (0,)), ((), ())), preferred_element_type=F32
    )
    back = lax.dot_general(
        fields[:, 2 * n_tok :], full[:, 2 * ff :], (((0,), (0,)), ((), ())), preferred_element_type=F32
    )
    gate_pre, up_pre = pre[:n_tok, :ff], pre[:n_tok, ff:]
    gate_tan, up_tan = pre[n_tok:, :ff], pre[n_tok:, ff:]
    held = slot_tokens[:, None] == lax.broadcasted_iota(jnp.int32, (slot_tokens.shape[0], n_tok), 1)
    gate = jnp.where(jnp.any(held, axis=0), gates, 0.0)
    back = gate[:, None] * back
    squash = jax.nn.sigmoid(gate_pre)
    first = squash * (1.0 + gate_pre * (1.0 - squash))
    second = squash * (1.0 - squash) * (2.0 + gate_pre * (1.0 - 2.0 * squash))
    gate_dir = (back * (up_tan * first + up_pre * second * gate_tan)).astype(BF)
    up_dir = (back * first * gate_tan).astype(BF)
    dirs = jnp.concatenate([gate_dir, up_dir], axis=1)
    sums = lax.dot_general(both, dirs, (((1,), (1,)), ((), ())), preferred_element_type=F32)

    sums = sums.reshape(NC, NY, NH, feat, n_tok)
    sums = take(sums, c) + other_core(take(sums, 1 - c))

    shares = lax.all_to_all(sums.astype(BF), "y", 0, 0, tiled=True).astype(F32)
    kept = jnp.sum(shares, axis=0)
    out = take(kept, zh) + other_half(take(kept, 1 - zh).astype(BF)).astype(F32)
    return out.T.astype(BF)


def solution(mesh):
    fine = Mesh(mesh.devices.reshape(NZ, NX, NH, NY, NC), ("zl", "x", "zh", "y", "c"))
    dp, tensor = ("zl", "x"), ("zh", "y", "c")
    tok = P(dp, tensor)
    in_specs = (tok, tok, tok, P(dp), P(dp), tok, tok, P(tensor, dp))
    return jax.shard_map(body, mesh=fine, in_specs=in_specs, out_specs=tok, check_vma=False)
```
